32 devices in a mesh: band: 4 (over z), dom: 8 (over y, x, core).
Axes of the slice: x: 2, y: 2, z: 4, core: 2. Of those that a mesh axis runs over, the one named last changes fastest.
Arguments:
- orbitals: float32 [128, 32, 12288], P('band', 'dom'), may hold values from -8 to 8
- potential: float32 [32, 12288], P('dom'), may hold values from -2 to 2
Outputs:
- updated: float32 [128, 32, 12288], P('band', 'dom')
The draws below stay inside these ranges and needn't reach their ends.
All inputs are finite; a program needn't handle non-finite values.
Results may differ from the reference program's by a relative error of at most 0.00012.
Values sent between devices are 32-bit elements; how exact they have to be, the bound alone decides.
A program may use at most 384 MiB of HBM per device.

```python
import jax
import jax.numpy as jnp
from jax import lax

BLOCK = 32
NY = 96
NZ = 128
ORBS = 128
NX = 32
PLANE = 12288


def draw_orbitals(key, part):
    subkeys = jax.random.split(key, 3)
    shape = (ORBS, NX, NY * NZ)
    noise_part = jax.random.normal(subkeys[0], shape, jnp.float32)
    mixing = jax.random.normal(subkeys[2], (ORBS, 4), jnp.float32) * 0.7
    shared = jax.random.normal(subkeys[1], (4, NX, NY * NZ), jnp.float32)
    combined = noise_part
    for column in range(4):
        combined = combined + mixing[:, column, None, None] * shared[column][None]
    return jnp.clip(combined, -8.0, 8.0)


def steps_of(stream_key, extent, pieces, smallest, largest):
    factor_of = 1.0
    for position, parts in pieces:
        steps = jax.random.uniform(jax.random.fold_in(jax.random.fold_in(stream_key, 6), position), (parts,), jnp.float32, smallest / len(pieces), largest / len(pieces))
        factor_of = factor_of * jnp.repeat(jnp.exp(steps), extent[position] // parts).reshape((-1,) + (1,) * (len(extent) - 1 - position))
    return factor_of


def setup_inputs(seed: int = 0) -> dict:
    key_list = jax.random.split(jax.random.key(seed), 3)
    return {
        "orbitals": draw_orbitals(jax.random.fold_in(key_list[2], 71), 0),
        "potential": jnp.clip(jax.random.uniform(key_list[1], (NX, PLANE), jnp.float32, -2.0, 2.0) * steps_of(key_list[1], (NX, PLANE), ((0, 8),), -0.4, 0.0), -2.0, 2.0),
    }


COEFFS = (-205.0 / 72.0, 8.0 / 5.0, -1.0 / 5.0, 8.0 / 315.0, -1.0 / 560.0)

def plane_laplacian(orbital, row_len):
    depth_index = lax.broadcasted_iota(jnp.int32, orbital.shape, orbital.ndim - 1) % row_len
    total = 2.0 * COEFFS[0] * orbital
    for offset in range(1, 5):
        beside_y = jnp.roll(orbital, offset * row_len, -1) + jnp.roll(orbital, -offset * row_len, -1)
        below_z = jnp.where(depth_index >= offset, jnp.roll(orbital, offset, -1), jnp.roll(orbital, offset - row_len, -1))
        above_z = jnp.where(depth_index < row_len - offset, jnp.roll(orbital, -offset, -1), jnp.roll(orbital, row_len - offset, -1))
        total = total + COEFFS[offset] * (beside_y + below_z + above_z)
    return total

def hamiltonian(orbital, potential):
    along_x = COEFFS[0] * orbital
    for offset in range(1, 5):
        along_x = along_x + COEFFS[offset] * (jnp.roll(orbital, offset, 0) + jnp.roll(orbital, -offset, 0))
    return -0.5 * (plane_laplacian(orbital, NZ) + along_x) + potential * orbital

def reference(orbitals, potential):
    applied = lax.map(lambda orbital: hamiltonian(orbital, potential), orbitals)
    flat_rows = applied.reshape(ORBS, -1)
    cell_count = NX * NY * NZ
    block_rows = flat_rows[:BLOCK]
    later_rows = flat_rows[BLOCK:]
    correlation = jnp.dot(block_rows, block_rows.T, precision=lax.Precision.HIGHEST) / cell_count
    lower_tri = jnp.linalg.cholesky(correlation)
    basis_rows = jax.scipy.linalg.solve_triangular(lower_tri, block_rows, lower=True)
    coeffs = jnp.dot(basis_rows, later_rows.T, precision=lax.Precision.HIGHEST) / cell_count
    projected = later_rows - jnp.dot(coeffs.T, basis_rows, precision=lax.Precision.HIGHEST)
    return jnp.concatenate([basis_rows, projected], axis=0).reshape(ORBS, NX, NY * NZ)
```

```python
import functools

import jax
import jax.numpy as jnp
from jax import lax
from jax.experimental import pallas as pl
from jax.experimental.pallas import tpu as pltpu
from jax.sharding import PartitionSpec as P

NZ = 128
WIDTH = 4
COEFFS = (-205.0 / 72.0, 8.0 / 5.0, -1.0 / 5.0, 8.0 / 315.0, -1.0 / 560.0)
HALF = tuple(-0.5 * c for c in COEFFS)
CHUNK_Y = 4
WINDOW = 4
MIB = 1024 * 1024
NT = (((1,), (1,)), ((), ()))
MESH = pl.DeviceIdType.MESH


def split(value):
    high = value.astype(jnp.bfloat16)
    low = (value - high.astype(jnp.float32)).astype(jnp.bfloat16)
    return high, low


def apply_kernel(
    nb, nd, planes, ny,
    x_ref, v_ref, a_out, b_out, g_out,
    nat, xs, from_left, from_right, own, blk, acc, part, parts,
    load_sem, halo_send, halo_recv, blk_send, blk_recv, a_sem, b_sem, part_send, part_recv, g_sem,
):
    block = xs.shape[1]
    rows = planes * ny
    chunk = planes * CHUNK_Y
    chunks = ny // CHUNK_Y
    band = lax.axis_index("band")
    dom = lax.axis_index("dom")
    right = lax.rem(dom + 1, nd)
    left = lax.rem(dom + nd - 1, nd)

    def load(c):
        span = pl.ds(pl.multiple_of(c * chunk, chunk), chunk)
        return pltpu.make_async_copy(x_ref.at[:, span, :], nat.at[:, span, :], load_sem.at[c])

    def halo(c, way):
        span = pl.ds(c * chunk, chunk)
        return pltpu.make_async_remote_copy(
            src_ref=xs.at[span],
            dst_ref=(from_left, from_right)[way].at[span],
            send_sem=halo_send.at[way, c],
            recv_sem=halo_recv.at[way, c],
            device_id=(band, (right, left)[way]),
            device_id_type=MESH,
        )

    def onward(c):
        span = pl.ds(c * chunk, chunk)
        return pltpu.make_async_remote_copy(
            src_ref=blk.at[span],
            dst_ref=blk.at[span],
            send_sem=blk_send.at[c],
            recv_sem=blk_recv.at[c],
            device_id=(lax.rem(band + 1, nb), dom),
            device_id_type=MESH,
        )

    def save(c, which):
        span = pl.ds(c * chunk, chunk)
        source, target, sem = ((own, a_out, a_sem), (blk, b_out, b_sem))[which]
        return pltpu.make_async_copy(source.at[span], target.at[span], sem.at[c])

    def total_to(step):
        peer = lax.rem(dom + step, nd)
        return pltpu.make_async_remote_copy(
            src_ref=part, dst_ref=parts.at[dom], send_sem=part_send.at[step],
            recv_sem=part_recv.at[dom], device_id=(band, peer), device_id_type=MESH,
        )

    def total_from(step):
        peer = lax.rem(dom + nd - step, nd)
        return pltpu.make_async_remote_copy(
            src_ref=part, dst_ref=parts.at[peer], send_sem=part_send.at[step],
            recv_sem=part_recv.at[peer], device_id=(band, peer), device_id_type=MESH,
        )

    @pl.loop(0, chunks)
    def _(c):
        load(c).start()

    barrier = pltpu.get_barrier_semaphore()
    for step in range(1, nd):
        pl.semaphore_signal(
            barrier, inc=1, device_id=(band, lax.rem(dom + step, nd)), device_id_type=MESH
        )

    for step in (1, nb - 1):
        pl.semaphore_signal(
            barrier, inc=1, device_id=(lax.rem(band + step, nb), dom), device_id_type=MESH
        )
    pl.semaphore_wait(barrier, nd + 1)

    acc[...] = jnp.zeros_like(acc)
    flat = nat.reshape(block * rows, NZ)

    @pl.loop(0, chunks)
    def _(c):
        load(c).wait()

        @pl.loop(0, chunk)
        def _(i):
            row = c * chunk + i
            xs[row] = flat[pl.ds(row, block, stride=rows), :]

        @pl.when(c < WINDOW)
        def _():
            halo(c, 0).start()
            halo(c, 1).start()

    def hamiltonian(c):
        @pl.loop(0, CHUNK_Y)
        def _(i):
            y = c * CHUNK_Y + i
            base = y * planes
            before = [lax.rem(y + ny - k, ny) * planes for k in range(WIDTH + 1)]
            after = [lax.rem(y + k, ny) * planes for k in range(WIDTH + 1)]

            def plane(p):
                if p < 0:
                    return from_left[base + planes + p]
                if p >= planes:
                    return from_right[base + p - planes]
                return xs[base + p]

            for p in range(planes):
                centre = xs[base + p]
                total = (v_ref[pl.ds(base + p, 1), :] + 3.0 * HALF[0]) * centre
                for k in range(1, WIDTH + 1):
                    near = (
                        (plane(p - k) + plane(p + k))
                        + (xs[before[k] + p] + xs[after[k] + p])
                        + (pltpu.roll(centre, k, 1) + pltpu.roll(centre, NZ - k, 1))
                    )
                    total = total + HALF[k] * near
                own[base + p] = total

                @pl.when(band == 0)
                def _():
                    blk[base + p] = total

    def gram(c):
        @pl.loop(0, CHUNK_Y)
        def _(i):
            base = (c * CHUNK_Y + i) * planes
            both = jnp.concatenate(
                [
                    jnp.concatenate([blk[base + p] for p in range(planes)], axis=1),
                    jnp.concatenate([own[base + p] for p in range(planes)], axis=1),
                ],
                axis=0,
            )
            high, low = split(both)
            lhs = jnp.concatenate([high, low], axis=0)
            rhs = jnp.concatenate([high[:block], low[:block]], axis=0)
            acc[...] += lax.dot_general(lhs, rhs, NT, preferred_element_type=jnp.float32)

    @pl.loop(0, chunks + nb - 1)
    def _(step):
        @pl.when(step < chunks)
        def _():
            @pl.when(step + WINDOW < chunks)
            def _():
                halo(step + WINDOW, 0).start()
                halo(step + WINDOW, 1).start()

            halo(step, 0).wait_recv()
            halo(step, 1).wait_recv()
            hamiltonian(step)

        c = step - band

        @pl.when(jnp.logical_and(c >= 0, c < chunks))
        def _():
            @pl.when(band > 0)
            def _():
                onward(c).wait_recv()

            @pl.when(band < nb - 1)
            def _():
                onward(c).start()

            save(c, 0).start()
            save(c, 1).start()
            gram(c)

    found = acc[...]
    found = found[: 2 * block] + found[2 * block :]
    found = found[:, :block] + found[:, block:]
    found = jnp.concatenate([found, jnp.zeros((2 * block, NZ - block), jnp.float32)], axis=1)
    part[...] = found
    for step in range(1, nd):
        total_to(step).start()
    parts[dom] = found
    for step in range(1, nd):
        total_from(step).wait_recv()
    summed = parts[0]
    for step in range(1, nd):
        summed = summed + parts[step]
    part_sum = summed

    @pl.loop(0, chunks)
    def _(c):
        halo(c, 0).wait_send()
        halo(c, 1).wait_send()
        save(c, 0).wait()
        save(c, 1).wait()

        @pl.when(band < nb - 1)
        def _():
            onward(c).wait_send()

    for step in range(1, nd):
        total_to(step).wait_send()
    part[...] = part_sum
    out = pltpu.make_async_copy(part, g_out, g_sem)
    out.start()
    out.wait()


def finish_kernel(count, planes, g_ref, a_ref, b_ref, o_ref, weights):
    block = a_ref.shape[1]
    rows = a_ref.shape[0]
    band = lax.axis_index("band")

    @pl.when(pl.program_id(0) == 0)
    def _():
        gram = g_ref[...] * (1.0 / count)
        corr = gram[:block, :block]
        cross = gram[block:, :block]
        row_id = lax.broadcasted_iota(jnp.int32, (block, block), 0)
        col_id = lax.broadcasted_iota(jnp.int32, (block, block), 1)
        work = jnp.concatenate([corr, jnp.where(row_id == col_id, 1.0, 0.0)], axis=1)
        row_of = lax.broadcasted_iota(jnp.int32, (block, 1), 0)
        for k in range(block):
            scale = 1.0 / jnp.sqrt(work[k : k + 1, k : k + 1])
            pivot = work[k : k + 1, :] * scale
            factor = jnp.where(row_of > k, work[:, k : k + 1] * scale, 0.0)
            work = jnp.where(row_of == k, pivot, work - factor * pivot)
        inverse = jnp.where(col_id <= row_id, work[:, block:], 0.0)
        exact = dict(precision=lax.Precision.HIGHEST, preferred_element_type=jnp.float32)
        coeffs = lax.dot_general(cross, inverse, NT, **exact)
        mixed = jnp.dot(coeffs, inverse, **exact)
        chosen = jnp.where(band == 0, -inverse, mixed)
        high, low = split(chosen)
        weights[...] = jnp.concatenate([high, low, high, low], axis=1)

    keep = jnp.where(band == 0, 0.0, 1.0).astype(jnp.float32)
    lhs = weights[...]
    flat = o_ref.reshape(block * rows, NZ)

    @pl.loop(0, rows // planes)
    def _(i):
        base = i * planes
        high, low = split(jnp.concatenate([b_ref[base + p] for p in range(planes)], axis=1))
        rhs = jnp.concatenate([high, high, low, low], axis=0)
        change = jnp.dot(lhs, rhs, preferred_element_type=jnp.float32)
        for p in range(planes):
            flat[pl.ds(base + p, block, stride=rows), :] = (
                keep * a_ref[base + p] - change[:, p * NZ : (p + 1) * NZ]
            )


def body(orbitals, potential):
    block, planes, plane = orbitals.shape
    ny = plane // NZ
    rows = planes * ny
    nb, nd = lax.axis_size("band"), lax.axis_size("dom")
    chunk_count = ny // CHUNK_Y
    x = orbitals.reshape(block, planes, ny, NZ).transpose(0, 2, 1, 3).reshape(block, rows, NZ)
    v = potential.reshape(planes, ny, NZ).transpose(1, 0, 2).reshape(rows, NZ)
    cells = jax.ShapeDtypeStruct((rows, block, NZ), jnp.float32)
    cells_vmem = pltpu.VMEM((rows, block, NZ), jnp.float32)
    dma = pltpu.SemaphoreType.DMA
    hbm = pl.BlockSpec(memory_space=pl.ANY)
    applied, basis, gram = pl.pallas_call(
        functools.partial(apply_kernel, nb, nd, planes, ny),
        out_shape=(cells, cells, jax.ShapeDtypeStruct((2 * block, NZ), jnp.float32)),
        in_specs=[hbm, pl.BlockSpec(memory_space=pltpu.VMEM)],
        out_specs=(hbm, hbm, hbm),
        scratch_shapes=[
            pltpu.VMEM((block, rows, NZ), jnp.float32),
            cells_vmem, cells_vmem, cells_vmem, cells_vmem, cells_vmem,
            pltpu.VMEM((4 * block, 2 * block), jnp.float32),
            pltpu.VMEM((2 * block, NZ), jnp.float32),
            pltpu.VMEM((nd, 2 * block, NZ), jnp.float32),
            dma((chunk_count,)), dma((2, chunk_count)), dma((2, chunk_count)),
            dma((chunk_count,)), dma((chunk_count,)), dma((chunk_count,)), dma((chunk_count,)),
            dma((nd,)), dma((nd,)), dma,
        ],
        compiler_params=pltpu.CompilerParams(
            collective_id=0, has_side_effects=True, vmem_limit_bytes=48 * MIB
        ),
        cost_estimate=pl.CostEstimate(
            flops=80 * block * rows * NZ, bytes_accessed=12 * block * rows * NZ, transcendentals=0
        ),
        name="apply_and_share",
    )(x, v)
    step_rows = 8 * planes
    count = rows * NZ * nd
    cell_spec = pl.BlockSpec((step_rows, block, NZ), lambda i: (i, 0, 0))
    result = pl.pallas_call(
        functools.partial(finish_kernel, count, planes),
        grid=(rows // step_rows,),
        out_shape=jax.ShapeDtypeStruct((block, rows, NZ), jnp.float32),
        in_specs=[pl.BlockSpec((2 * block, NZ), lambda i: (0, 0)), cell_spec, cell_spec],
        out_specs=pl.BlockSpec((block, step_rows, NZ), lambda i: (0, i, 0)),
        scratch_shapes=[pltpu.VMEM((block, 4 * block), jnp.bfloat16)],
        compiler_params=pltpu.CompilerParams(vmem_limit_bytes=56 * MIB),
        cost_estimate=pl.CostEstimate(
            flops=80 * block * rows * NZ, bytes_accessed=12 * block * rows * NZ, transcendentals=0
        ),
        name="finish",
    )(gram, applied, basis)
    result = result.reshape(block, ny, planes, NZ).transpose(0, 2, 1, 3)
    return result.reshape(block, planes, plane)


def solution(mesh):
    placed = (P("band", "dom", None), P("dom", None))
    return jax.shard_map(
        body, mesh=mesh, in_specs=placed, out_specs=P("band", "dom", None), check_vma=False
    )
```

```python
import functools

import jax
import jax.numpy as jnp
from jax import lax
from jax.experimental import pallas as pl
from jax.experimental.pallas import tpu as pltpu
from jax.sharding import PartitionSpec as P

NZ = 128
WIDTH = 4
COEFFS = (-205.0 / 72.0, 8.0 / 5.0, -1.0 / 5.0, 8.0 / 315.0, -1.0 / 560.0)
HALF = tuple(-0.5 * c for c in COEFFS)
CHUNK_Y = 2
WINDOW = 8
MIB = 1024 * 1024
NT = (((1,), (1,)), ((), ()))
MESH = pl.DeviceIdType.MESH


def split(value):
    high = value.astype(jnp.bfloat16)
    low = (value - high.astype(jnp.float32)).astype(jnp.bfloat16)
    return high, low


def apply_kernel(
    nb, nd, planes, ny,
    x_ref, v_hbm, a_out, b_out, g_out,
    nat, xs, from_left, from_right, own, blk, v_ref, acc, part, parts,
    load_sem, halo_send, halo_recv, blk_send, blk_recv, a_sem, b_sem, part_send, part_recv, g_sem, v_sem,
):
    block = xs.shape[1]
    rows = planes * ny
    chunk = planes * CHUNK_Y
    chunks = ny // CHUNK_Y
    band = lax.axis_index("band")
    dom = lax.axis_index("dom")
    right = lax.rem(dom + 1, nd)
    left = lax.rem(dom + nd - 1, nd)

    def load(c):
        span = pl.ds(pl.multiple_of(c * chunk, chunk), chunk)
        return pltpu.make_async_copy(x_ref.at[:, span, :], nat.at[:, span, :], load_sem.at[c])

    def halo(c, way):
        span = pl.ds(c * chunk, chunk)
        return pltpu.make_async_remote_copy(
            src_ref=xs.at[span],
            dst_ref=(from_left, from_right)[way].at[span],
            send_sem=halo_send.at[way, c],
            recv_sem=halo_recv.at[way, c],
            device_id=(band, (right, left)[way]),
            device_id_type=MESH,
        )

    def onward(c):
        span = pl.ds(c * chunk, chunk)
        return pltpu.make_async_remote_copy(
            src_ref=blk.at[span],
            dst_ref=blk.at[span],
            send_sem=blk_send.at[c],
            recv_sem=blk_recv.at[c],
            device_id=(lax.rem(band + 1, nb), dom),
            device_id_type=MESH,
        )

    def save(c, which):
        span = pl.ds(c * chunk, chunk)
        source, target, sem = ((own, a_out, a_sem), (blk, b_out, b_sem))[which]
        return pltpu.make_async_copy(source.at[span], target.at[span], sem.at[c])

    def total_to(step):
        peer = lax.rem(dom + step, nd)
        return pltpu.make_async_remote_copy(
            src_ref=part, dst_ref=parts.at[dom], send_sem=part_send.at[step],
            recv_sem=part_recv.at[dom], device_id=(band, peer), device_id_type=MESH,
        )

    def total_from(step):
        peer = lax.rem(dom + nd - step, nd)
        return pltpu.make_async_remote_copy(
            src_ref=part, dst_ref=parts.at[peer], send_sem=part_send.at[step],
            recv_sem=part_recv.at[peer], device_id=(band, peer), device_id_type=MESH,
        )

    @pl.loop(0, chunks)
    def _(c):
        load(c).start()

    potential = pltpu.make_async_copy(v_hbm, v_ref, v_sem)
    potential.start()

    barrier = pltpu.get_barrier_semaphore()
    for step in range(1, nd):
        pl.semaphore_signal(
            barrier, inc=1, device_id=(band, lax.rem(dom + step, nd)), device_id_type=MESH
        )

    for step in (1, nb - 1):
        pl.semaphore_signal(
            barrier, inc=1, device_id=(lax.rem(band + step, nb), dom), device_id_type=MESH
        )
    pl.semaphore_wait(barrier, nd + 1)

    acc[...] = jnp.zeros_like(acc)
    flat = nat.reshape(block * rows, NZ)

    @pl.loop(0, chunks)
    def _(c):
        load(c).wait()

        @pl.loop(0, chunk)
        def _(i):
            row = c * chunk + i
            xs[row] = flat[pl.ds(row, block, stride=rows), :]

        @pl.when(c < WINDOW)
        def _():
            halo(c, 0).start()
            halo(c, 1).start()

    potential.wait()

    def hamiltonian(c):
        @pl.loop(0, CHUNK_Y)
        def _(i):
            y = c * CHUNK_Y + i
            base = y * planes
            before = [lax.rem(y + ny - k, ny) * planes for k in range(WIDTH + 1)]
            after = [lax.rem(y + k, ny) * planes for k in range(WIDTH + 1)]

            def plane(p):
                if p < 0:
                    return from_left[base + planes + p]
                if p >= planes:
                    return from_right[base + p - planes]
                return xs[base + p]

            for p in range(planes):
                centre = xs[base + p]
                total = (v_ref[pl.ds(base + p, 1), :] + 3.0 * HALF[0]) * centre
                for k in range(1, WIDTH + 1):
                    near = (
                        (plane(p - k) + plane(p + k))
                        + (xs[before[k] + p] + xs[after[k] + p])
                        + (pltpu.roll(centre, k, 1) + pltpu.roll(centre, NZ - k, 1))
                    )
                    total = total + HALF[k] * near
                own[base + p] = total

                @pl.when(band == 0)
                def _():
                    blk[base + p] = total

    def gram(c):
        @pl.loop(0, CHUNK_Y)
        def _(i):
            base = (c * CHUNK_Y + i) * planes
            both = jnp.concatenate(
                [
                    jnp.concatenate([blk[base + p] for p in range(planes)], axis=1),
                    jnp.concatenate([own[base + p] for p in range(planes)], axis=1),
                ],
                axis=0,
            )
            high, low = split(both)
            lhs = jnp.concatenate([high, low], axis=0)
            rhs = jnp.concatenate([high[:block], low[:block]], axis=0)
            acc[...] += lax.dot_general(lhs, rhs, NT, preferred_element_type=jnp.float32)

    @pl.loop(0, chunks + nb - 1)
    def _(step):
        @pl.when(step < chunks)
        def _():
            @pl.when(step + WINDOW < chunks)
            def _():
                halo(step + WINDOW, 0).start()
                halo(step + WINDOW, 1).start()

            halo(step, 0).wait_recv()
            halo(step, 1).wait_recv()
            hamiltonian(step)

        c = step - band

        @pl.when(jnp.logical_and(c >= 0, c < chunks))
        def _():
            @pl.when(band > 0)
            def _():
                onward(c).wait_recv()

            @pl.when(band < nb - 1)
            def _():
                onward(c).start()

            save(c, 0).start()
            save(c, 1).start()
            gram(c)

    found = acc[...]
    found = found[: 2 * block] + found[2 * block :]
    found = found[:, :block] + found[:, block:]
    found = jnp.concatenate([found, jnp.zeros((2 * block, NZ - block), jnp.float32)], axis=1)
    part[...] = found
    for step in range(1, nd):
        total_to(step).start()
    parts[dom] = found
    for step in range(1, nd):
        total_from(step).wait_recv()
    summed = parts[0]
    for step in range(1, nd):
        summed = summed + parts[step]
    part_sum = summed

    @pl.loop(0, chunks)
    def _(c):
        halo(c, 0).wait_send()
        halo(c, 1).wait_send()
        save(c, 0).wait()
        save(c, 1).wait()

        @pl.when(band < nb - 1)
        def _():
            onward(c).wait_send()

    for step in range(1, nd):
        total_to(step).wait_send()
    part[...] = part_sum
    out = pltpu.make_async_copy(part, g_out, g_sem)
    out.start()
    out.wait()


def finish_kernel(count, planes, g_ref, a_ref, b_ref, o_ref, weights):
    block = a_ref.shape[1]
    rows = a_ref.shape[0]
    band = lax.axis_index("band")

    @pl.when(pl.program_id(0) == 0)
    def _():
        gram = g_ref[...] * (1.0 / count)
        corr = gram[:block, :block]
        cross = gram[block:, :block]
        row_id = lax.broadcasted_iota(jnp.int32, (block, block), 0)
        col_id = lax.broadcasted_iota(jnp.int32, (block, block), 1)
        work = jnp.concatenate([corr, jnp.where(row_id == col_id, 1.0, 0.0)], axis=1)
        row_of = lax.broadcasted_iota(jnp.int32, (block, 1), 0)
        for k in range(block):
            pivot = work[k : k + 1, :]
            factor = jnp.where(row_of > k, work[:, k : k + 1] / pivot[:, k : k + 1], 0.0)
            work = work - factor * pivot
        diagonal = jnp.where(row_id == col_id, work[:, :block], 0.0)
        norm = jnp.sqrt(jnp.sum(diagonal, axis=1, keepdims=True))
        inverse = jnp.where(col_id <= row_id, work[:, block:] / norm, 0.0)
        exact = dict(precision=lax.Precision.HIGHEST, preferred_element_type=jnp.float32)
        coeffs = lax.dot_general(cross, inverse, NT, **exact)
        mixed = jnp.dot(coeffs, inverse, **exact)
        chosen = jnp.where(band == 0, -inverse, mixed)
        high, low = split(chosen)
        weights[...] = jnp.concatenate([high, low, high, low], axis=1)

    keep = jnp.where(band == 0, 0.0, 1.0).astype(jnp.float32)
    lhs = weights[...]

    @pl.loop(0, rows // 8, unroll=2)
    def _(i):
        base = pl.multiple_of(i * 8, 8)
        cells = [base + p for p in range(8)]
        high, low = split(jnp.concatenate([b_ref[cell] for cell in cells], axis=1))
        rhs = jnp.concatenate([high, high, low, low], axis=0)
        change = jnp.dot(lhs, rhs, preferred_element_type=jnp.float32)
        fresh = [
            keep * a_ref[cell] - change[:, p * NZ : (p + 1) * NZ]
            for p, cell in enumerate(cells)
        ]
        o_ref[:, pl.ds(base, 8), :] = jnp.swapaxes(jnp.stack(fresh), 0, 1)


def body(orbitals, potential):
    block, planes, plane = orbitals.shape
    ny = plane // NZ
    rows = planes * ny
    nb, nd = lax.axis_size("band"), lax.axis_size("dom")
    chunk_count = ny // CHUNK_Y
    x = orbitals.reshape(block, planes, ny, NZ).transpose(0, 2, 1, 3).reshape(block, rows, NZ)
    v = potential.reshape(planes, ny, NZ).transpose(1, 0, 2).reshape(rows, NZ)
    cells = jax.ShapeDtypeStruct((rows, block, NZ), jnp.float32)
    cells_vmem = pltpu.VMEM((rows, block, NZ), jnp.float32)
    dma = pltpu.SemaphoreType.DMA
    hbm = pl.BlockSpec(memory_space=pl.ANY)
    applied, basis, gram = pl.pallas_call(
        functools.partial(apply_kernel, nb, nd, planes, ny),
        out_shape=(cells, cells, jax.ShapeDtypeStruct((2 * block, NZ), jnp.float32)),
        in_specs=[hbm, hbm],
        out_specs=(hbm, hbm, hbm),
        scratch_shapes=[
            pltpu.VMEM((block, rows, NZ), jnp.float32),
            cells_vmem, cells_vmem, cells_vmem, cells_vmem, cells_vmem,
            pltpu.VMEM((rows, NZ), jnp.float32),
            pltpu.VMEM((4 * block, 2 * block), jnp.float32),
            pltpu.VMEM((2 * block, NZ), jnp.float32),
            pltpu.VMEM((nd, 2 * block, NZ), jnp.float32),
            dma((chunk_count,)), dma((2, chunk_count)), dma((2, chunk_count)),
            dma((chunk_count,)), dma((chunk_count,)), dma((chunk_count,)), dma((chunk_count,)),
            dma((nd,)), dma((nd,)), dma, dma,
        ],
        compiler_params=pltpu.CompilerParams(
            collective_id=0, has_side_effects=True, vmem_limit_bytes=60 * MIB
        ),
        cost_estimate=pl.CostEstimate(
            flops=80 * block * rows * NZ, bytes_accessed=12 * block * rows * NZ, transcendentals=0
        ),
        name="apply_and_share",
    )(x, v)
    step_rows = 8 * planes
    count = rows * NZ * nd
    cell_spec = pl.BlockSpec((step_rows, block, NZ), lambda i: (i, 0, 0))
    result = pl.pallas_call(
        functools.partial(finish_kernel, count, planes),
        grid=(rows // step_rows,),
        out_shape=jax.ShapeDtypeStruct((block, rows, NZ), jnp.float32),
        in_specs=[pl.BlockSpec((2 * block, NZ), lambda i: (0, 0)), cell_spec, cell_spec],
        out_specs=pl.BlockSpec((block, step_rows, NZ), lambda i: (0, i, 0)),
        scratch_shapes=[pltpu.VMEM((block, 4 * block), jnp.bfloat16)],
        compiler_params=pltpu.CompilerParams(vmem_limit_bytes=60 * MIB),
        cost_estimate=pl.CostEstimate(
            flops=80 * block * rows * NZ, bytes_accessed=12 * block * rows * NZ, transcendentals=0
        ),
        name="finish",
    )(gram, applied, basis)
    result = result.reshape(block, ny, planes, NZ).transpose(0, 2, 1, 3)
    return result.reshape(block, planes, plane)


def solution(mesh):
    placed = (P("band", "dom", None), P("dom", None))
    return jax.shard_map(
        body, mesh=mesh, in_specs=placed, out_specs=P("band", "dom", None), check_vma=False
    )
```

```python
import functools

import jax
import jax.numpy as jnp
from jax import lax
from jax.experimental import pallas as pl
from jax.experimental.pallas import tpu as pltpu
from jax.sharding import PartitionSpec as P

NZ = 128
WIDTH = 4
COEFFS = (-205.0 / 72.0, 8.0 / 5.0, -1.0 / 5.0, 8.0 / 315.0, -1.0 / 560.0)
HALF = tuple(-0.5 * c for c in COEFFS)
CHUNK_Y = 2
WINDOW = 4
MIB = 1024 * 1024
NT = (((1,), (1,)), ((), ()))
MESH = pl.DeviceIdType.MESH


def split(value):
    high = value.astype(jnp.bfloat16)
    low = (value - high.astype(jnp.float32)).astype(jnp.bfloat16)
    return high, low


def apply_kernel(
    nb, nd, planes, ny,
    x_ref, v_hbm, a_out, b_out, g_out,
    nat, xs, from_left, from_right, own, blk, v_ref, acc, part, parts,
    load_sem, halo_send, halo_recv, blk_send, blk_recv, a_sem, b_sem, part_send, part_recv, g_sem, v_sem,
):
    block = xs.shape[1]
    rows = planes * ny
    chunk = planes * CHUNK_Y
    chunks = ny // CHUNK_Y
    band = lax.axis_index("band")
    dom = lax.axis_index("dom")
    right = lax.rem(dom + 1, nd)
    left = lax.rem(dom + nd - 1, nd)

    def load(c):
        span = pl.ds(pl.multiple_of(c * chunk, chunk), chunk)
        return pltpu.make_async_copy(x_ref.at[:, span, :], nat.at[:, span, :], load_sem.at[c])

    def halo(c, way):
        span = pl.ds(c * chunk, chunk)
        return pltpu.make_async_remote_copy(
            src_ref=xs.at[span],
            dst_ref=(from_left, from_right)[way].at[span],
            send_sem=halo_send.at[way, c],
            recv_sem=halo_recv.at[way, c],
            device_id=(band, (right, left)[way]),
            device_id_type=MESH,
        )

    def onward(c):
        span = pl.ds(c * chunk, chunk)
        return pltpu.make_async_remote_copy(
            src_ref=blk.at[span],
            dst_ref=blk.at[span],
            send_sem=blk_send.at[c],
            recv_sem=blk_recv.at[c],
            device_id=(lax.rem(band + 1, nb), dom),
            device_id_type=MESH,
        )

    def save(c, which):
        span = pl.ds(c * chunk, chunk)
        source, target, sem = ((own, a_out, a_sem), (blk, b_out, b_sem))[which]
        return pltpu.make_async_copy(source.at[span], target.at[span], sem.at[c])

    def total_to(step):
        peer = lax.rem(dom + step, nd)
        return pltpu.make_async_remote_copy(
            src_ref=part, dst_ref=parts.at[dom], send_sem=part_send.at[step],
            recv_sem=part_recv.at[dom], device_id=(band, peer), device_id_type=MESH,
        )

    def total_from(step):
        peer = lax.rem(dom + nd - step, nd)
        return pltpu.make_async_remote_copy(
            src_ref=part, dst_ref=parts.at[peer], send_sem=part_send.at[step],
            recv_sem=part_recv.at[peer], device_id=(band, peer), device_id_type=MESH,
        )

    wrapped = -(-WIDTH // CHUNK_Y)

    def prepare(c):
        load(c).wait()

        @pl.loop(0, chunk // 8)
        def _(i):
            span = pl.ds(pl.multiple_of(c * chunk + i * 8, 8), 8)
            xs[span] = jnp.swapaxes(nat[:, span, :], 0, 1)

    for c in range(chunks - wrapped, chunks):
        load(c).start()

    @pl.loop(0, chunks - wrapped)
    def _(c):
        load(c).start()

    potential = pltpu.make_async_copy(v_hbm, v_ref, v_sem)
    potential.start()

    barrier = pltpu.get_barrier_semaphore()
    for step in range(1, nd):
        pl.semaphore_signal(
            barrier, inc=1, device_id=(band, lax.rem(dom + step, nd)), device_id_type=MESH
        )

    for step in (1, nb - 1):
        pl.semaphore_signal(
            barrier, inc=1, device_id=(lax.rem(band + step, nb), dom), device_id_type=MESH
        )
    pl.semaphore_wait(barrier, nd + 1)

    acc[...] = jnp.zeros_like(acc)

    @pl.loop(0, WINDOW)
    def _(c):
        prepare(c)
        halo(c, 0).start()
        halo(c, 1).start()

    for c in range(chunks - wrapped, chunks):
        prepare(c)
    potential.wait()

    def hamiltonian(c):
        @pl.loop(0, CHUNK_Y)
        def _(i):
            y = c * CHUNK_Y + i
            base = y * planes
            before = [lax.rem(y + ny - k, ny) * planes for k in range(WIDTH + 1)]
            after = [lax.rem(y + k, ny) * planes for k in range(WIDTH + 1)]

            def plane(p):
                if p < 0:
                    return from_left[base + planes + p]
                if p >= planes:
                    return from_right[base + p - planes]
                return xs[base + p]

            for p in range(planes):
                centre = xs[base + p]
                total = (v_ref[pl.ds(base + p, 1), :] + 3.0 * HALF[0]) * centre
                for k in range(1, WIDTH + 1):
                    near = (
                        (plane(p - k) + plane(p + k))
                        + (xs[before[k] + p] + xs[after[k] + p])
                        + (pltpu.roll(centre, k, 1) + pltpu.roll(centre, NZ - k, 1))
                    )
                    total = total + HALF[k] * near
                own[base + p] = total

                @pl.when(band == 0)
                def _():
                    blk[base + p] = total

    def gram(c):
        @pl.loop(0, CHUNK_Y)
        def _(i):
            base = (c * CHUNK_Y + i) * planes
            both = jnp.concatenate(
                [
                    jnp.concatenate([blk[base + p] for p in range(planes)], axis=1),
                    jnp.concatenate([own[base + p] for p in range(planes)], axis=1),
                ],
                axis=0,
            )
            high, low = split(both)
            lhs = jnp.concatenate([high, low], axis=0)
            rhs = jnp.concatenate([high[:block], low[:block]], axis=0)
            acc[...] += lax.dot_general(lhs, rhs, NT, preferred_element_type=jnp.float32)

    @pl.loop(0, chunks + nb - 1)
    def _(step):
        @pl.when(step < chunks)
        def _():
            halo(step, 0).wait_recv()
            halo(step, 1).wait_recv()
            hamiltonian(step)

        c = step - band

        @pl.when(jnp.logical_and(c >= 0, c < chunks))
        def _():
            @pl.when(band > 0)
            def _():
                onward(c).wait_recv()

            @pl.when(band < nb - 1)
            def _():
                onward(c).start()

            save(c, 0).start()
            save(c, 1).start()
            gram(c)

        ahead = step + WINDOW

        @pl.when(ahead < chunks - wrapped)
        def _():
            prepare(ahead)

        @pl.when(ahead < chunks)
        def _():
            halo(ahead, 0).start()
            halo(ahead, 1).start()

    found = acc[...]
    found = found[: 2 * block] + found[2 * block :]
    found = found[:, :block] + found[:, block:]
    found = jnp.concatenate([found, jnp.zeros((2 * block, NZ - block), jnp.float32)], axis=1)
    part[...] = found
    for step in range(1, nd):
        total_to(step).start()
    parts[dom] = found
    for step in range(1, nd):
        total_from(step).wait_recv()
    summed = parts[0]
    for step in range(1, nd):
        summed = summed + parts[step]
    part_sum = summed

    @pl.loop(0, chunks)
    def _(c):
        halo(c, 0).wait_send()
        halo(c, 1).wait_send()
        save(c, 0).wait()
        save(c, 1).wait()

        @pl.when(band < nb - 1)
        def _():
            onward(c).wait_send()

    for step in range(1, nd):
        total_to(step).wait_send()
    part[...] = part_sum
    out = pltpu.make_async_copy(part, g_out, g_sem)
    out.start()
    out.wait()


def finish_kernel(count, planes, g_ref, a_ref, b_ref, o_ref, weights):
    block = a_ref.shape[1]
    rows = a_ref.shape[0]
    band = lax.axis_index("band")

    @pl.when(pl.program_id(0) == 0)
    def _():
        gram = g_ref[...] * (1.0 / count)
        corr = gram[:block, :block]
        cross = gram[block:, :block]
        row_id = lax.broadcasted_iota(jnp.int32, (block, block), 0)
        col_id = lax.broadcasted_iota(jnp.int32, (block, block), 1)
        work = jnp.concatenate([corr, jnp.where(row_id == col_id, 1.0, 0.0)], axis=1)
        row_of = lax.broadcasted_iota(jnp.int32, (block, 1), 0)
        for k in range(block):
            pivot = work[k : k + 1, :]
            factor = jnp.where(row_of > k, work[:, k : k + 1] / pivot[:, k : k + 1], 0.0)
            work = work - factor * pivot
        diagonal = jnp.where(row_id == col_id, work[:, :block], 0.0)
        norm = jnp.sqrt(jnp.sum(diagonal, axis=1, keepdims=True))
        inverse = jnp.where(col_id <= row_id, work[:, block:] / norm, 0.0)
        exact = dict(precision=lax.Precision.HIGHEST, preferred_element_type=jnp.float32)
        coeffs = lax.dot_general(cross, inverse, NT, **exact)
        mixed = jnp.dot(coeffs, inverse, **exact)
        chosen = jnp.where(band == 0, -inverse, mixed)
        high, low = split(chosen)
        weights[...] = jnp.concatenate([high, low, high, low], axis=1)

    keep = jnp.where(band == 0, 0.0, 1.0).astype(jnp.float32)
    lhs = weights[...]

    @pl.loop(0, rows // 8, unroll=2)
    def _(i):
        base = pl.multiple_of(i * 8, 8)
        cells = [base + p for p in range(8)]
        high, low = split(jnp.concatenate([b_ref[cell] for cell in cells], axis=1))
        rhs = jnp.concatenate([high, high, low, low], axis=0)
        change = jnp.dot(lhs, rhs, preferred_element_type=jnp.float32)
        fresh = [
            keep * a_ref[cell] - change[:, p * NZ : (p + 1) * NZ]
            for p, cell in enumerate(cells)
        ]
        o_ref[:, pl.ds(base, 8), :] = jnp.swapaxes(jnp.stack(fresh), 0, 1)


def body(orbitals, potential):
    block, planes, plane = orbitals.shape
    ny = plane // NZ
    rows = planes * ny
    nb, nd = lax.axis_size("band"), lax.axis_size("dom")
    chunk_count = ny // CHUNK_Y
    x = orbitals.reshape(block, planes, ny, NZ).transpose(0, 2, 1, 3).reshape(block, rows, NZ)
    v = potential.reshape(planes, ny, NZ).transpose(1, 0, 2).reshape(rows, NZ)
    cells = jax.ShapeDtypeStruct((rows, block, NZ), jnp.float32)
    cells_vmem = pltpu.VMEM((rows, block, NZ), jnp.float32)
    dma = pltpu.SemaphoreType.DMA
    hbm = pl.BlockSpec(memory_space=pl.ANY)
    applied, basis, gram = pl.pallas_call(
        functools.partial(apply_kernel, nb, nd, planes, ny),
        out_shape=(cells, cells, jax.ShapeDtypeStruct((2 * block, NZ), jnp.float32)),
        in_specs=[hbm, hbm],
        out_specs=(hbm, hbm, hbm),
        scratch_shapes=[
            pltpu.VMEM((block, rows, NZ), jnp.float32),
            cells_vmem, cells_vmem, cells_vmem, cells_vmem, cells_vmem,
            pltpu.VMEM((rows, NZ), jnp.float32),
            pltpu.VMEM((4 * block, 2 * block), jnp.float32),
            pltpu.VMEM((2 * block, NZ), jnp.float32),
            pltpu.VMEM((nd, 2 * block, NZ), jnp.float32),
            dma((chunk_count,)), dma((2, chunk_count)), dma((2, chunk_count)),
            dma((chunk_count,)), dma((chunk_count,)), dma((chunk_count,)), dma((chunk_count,)),
            dma((nd,)), dma((nd,)), dma, dma,
        ],
        compiler_params=pltpu.CompilerParams(
            collective_id=0, has_side_effects=True, vmem_limit_bytes=60 * MIB
        ),
        cost_estimate=pl.CostEstimate(
            flops=80 * block * rows * NZ, bytes_accessed=12 * block * rows * NZ, transcendentals=0
        ),
        name="apply_and_share",
    )(x, v)
    step_rows = 16 * planes
    count = rows * NZ * nd
    cell_spec = pl.BlockSpec((step_rows, block, NZ), lambda i: (i, 0, 0))
    result = pl.pallas_call(
        functools.partial(finish_kernel, count, planes),
        grid=(rows // step_rows,),
        out_shape=jax.ShapeDtypeStruct((block, rows, NZ), jnp.float32),
        in_specs=[pl.BlockSpec((2 * block, NZ), lambda i: (0, 0)), cell_spec, cell_spec],
        out_specs=pl.BlockSpec((block, step_rows, NZ), lambda i: (0, i, 0)),
        scratch_shapes=[pltpu.VMEM((block, 4 * block), jnp.bfloat16)],
        compiler_params=pltpu.CompilerParams(vmem_limit_bytes=60 * MIB),
        cost_estimate=pl.CostEstimate(
            flops=80 * block * rows * NZ, bytes_accessed=12 * block * rows * NZ, transcendentals=0
        ),
        name="finish",
    )(gram, applied, basis)
    result = result.reshape(block, ny, planes, NZ).transpose(0, 2, 1, 3)
    return result.reshape(block, planes, plane)


def solution(mesh):
    placed = (P("band", "dom", None), P("dom", None))
    return jax.shard_map(
        body, mesh=mesh, in_specs=placed, out_specs=P("band", "dom", None), check_vma=False
    )
```

```python
import functools

import jax
import jax.numpy as jnp
from jax import lax
from jax.experimental import pallas as pl
from jax.experimental.pallas import tpu as pltpu
from jax.sharding import PartitionSpec as P

NZ = 128
WIDTH = 4
COEFFS = (-205.0 / 72.0, 8.0 / 5.0, -1.0 / 5.0, 8.0 / 315.0, -1.0 / 560.0)
HALF = tuple(-0.5 * c for c in COEFFS)
CHUNK_Y = 2
WINDOW = 4
MIB = 1024 * 1024
NT = (((1,), (1,)), ((), ()))
MESH = pl.DeviceIdType.MESH


def split(value):
    high = value.astype(jnp.bfloat16)
    low = (value - high.astype(jnp.float32)).astype(jnp.bfloat16)
    return high, low


def apply_kernel(
    nb, nd, planes, ny,
    x_ref, v_hbm, a_out, b_out, g_out,
    nat, xs, from_left, from_right, own, blk, v_ref, acc, part, parts,
    load_sem, halo_send, halo_recv, blk_send, blk_recv, a_sem, b_sem, part_send, part_recv, g_sem, v_sem,
):
    block = xs.shape[1]
    rows = planes * ny
    chunk = planes * CHUNK_Y
    chunks = ny // CHUNK_Y
    band = lax.axis_index("band")
    dom = lax.axis_index("dom")
    right = lax.rem(dom + 1, nd)
    left = lax.rem(dom + nd - 1, nd)

    def load(c):
        span = pl.ds(pl.multiple_of(c * chunk, chunk), chunk)
        return pltpu.make_async_copy(x_ref.at[:, span, :], nat.at[:, span, :], load_sem.at[c])

    def halo(c, way):
        span = pl.ds(c * chunk, chunk)
        return pltpu.make_async_remote_copy(
            src_ref=xs.at[span],
            dst_ref=(from_left, from_right)[way].at[span],
            send_sem=halo_send.at[way, c],
            recv_sem=halo_recv.at[way, c],
            device_id=(band, (right, left)[way]),
            device_id_type=MESH,
        )

    def onward(c):
        span = pl.ds(c * chunk, chunk)
        return pltpu.make_async_remote_copy(
            src_ref=blk.at[span],
            dst_ref=blk.at[span],
            send_sem=blk_send.at[c],
            recv_sem=blk_recv.at[c],
            device_id=(lax.rem(band + 1, nb), dom),
            device_id_type=MESH,
        )

    def save(c, which):
        span = pl.ds(c * chunk, chunk)
        source, target, sem = ((own, a_out, a_sem), (blk, b_out, b_sem))[which]
        return pltpu.make_async_copy(source.at[span], target.at[span], sem.at[c])

    def total_to(step):
        peer = lax.rem(dom + step, nd)
        return pltpu.make_async_remote_copy(
            src_ref=part, dst_ref=parts.at[dom], send_sem=part_send.at[step],
            recv_sem=part_recv.at[dom], device_id=(band, peer), device_id_type=MESH,
        )

    def total_from(step):
        peer = lax.rem(dom + nd - step, nd)
        return pltpu.make_async_remote_copy(
            src_ref=part, dst_ref=parts.at[peer], send_sem=part_send.at[step],
            recv_sem=part_recv.at[peer], device_id=(band, peer), device_id_type=MESH,
        )

    wrapped = -(-WIDTH // CHUNK_Y)

    def prepare(c):
        load(c).wait()

        @pl.loop(0, chunk // 8)
        def _(i):
            span = pl.ds(pl.multiple_of(c * chunk + i * 8, 8), 8)
            xs[span] = jnp.swapaxes(nat[:, span, :], 0, 1)

    for c in range(chunks - wrapped, chunks):
        load(c).start()

    @pl.loop(0, chunks - wrapped)
    def _(c):
        load(c).start()

    potential = pltpu.make_async_copy(v_hbm, v_ref, v_sem)
    potential.start()

    barrier = pltpu.get_barrier_semaphore()
    for step in range(1, nd):
        pl.semaphore_signal(
            barrier, inc=1, device_id=(band, lax.rem(dom + step, nd)), device_id_type=MESH
        )

    for step in (1, nb - 1):
        pl.semaphore_signal(
            barrier, inc=1, device_id=(lax.rem(band + step, nb), dom), device_id_type=MESH
        )
    pl.semaphore_wait(barrier, nd + 1)

    acc[...] = jnp.zeros_like(acc)

    @pl.loop(0, WINDOW)
    def _(c):
        prepare(c)
        halo(c, 0).start()
        halo(c, 1).start()

    for c in range(chunks - wrapped, chunks):
        prepare(c)
    potential.wait()

    def hamiltonian(c):
        @pl.loop(0, CHUNK_Y)
        def _(i):
            y = c * CHUNK_Y + i
            base = y * planes
            before = [lax.rem(y + ny - k, ny) * planes for k in range(WIDTH + 1)]
            after = [lax.rem(y + k, ny) * planes for k in range(WIDTH + 1)]

            def plane(p):
                if p < 0:
                    return from_left[base + planes + p]
                if p >= planes:
                    return from_right[base + p - planes]
                return xs[base + p]

            for p in range(planes):
                centre = xs[base + p]
                total = (v_ref[pl.ds(base + p, 1), :] + 3.0 * HALF[0]) * centre
                for k in range(1, WIDTH + 1):
                    near = (
                        (plane(p - k) + plane(p + k))
                        + (xs[before[k] + p] + xs[after[k] + p])
                        + (pltpu.roll(centre, k, 1) + pltpu.roll(centre, NZ - k, 1))
                    )
                    total = total + HALF[k] * near
                own[base + p] = total

                @pl.when(band == 0)
                def _():
                    blk[base + p] = total

    def gram(c):
        @pl.loop(0, CHUNK_Y)
        def _(i):
            base = (c * CHUNK_Y + i) * planes
            both = jnp.concatenate(
                [
                    jnp.concatenate([blk[base + p] for p in range(planes)], axis=1),
                    jnp.concatenate([own[base + p] for p in range(planes)], axis=1),
                ],
                axis=0,
            )
            high, low = split(both)
            lhs = jnp.concatenate([high, low], axis=0)
            rhs = jnp.concatenate([high[:block], low[:block]], axis=0)
            acc[...] += lax.dot_general(lhs, rhs, NT, preferred_element_type=jnp.float32)

    @pl.loop(0, chunks + nb - 1)
    def _(step):
        @pl.when(step < chunks)
        def _():
            halo(step, 0).wait_recv()
            halo(step, 1).wait_recv()
            hamiltonian(step)

        c = step - band

        @pl.when(jnp.logical_and(c >= 0, c < chunks))
        def _():
            @pl.when(band > 0)
            def _():
                onward(c).wait_recv()

            @pl.when(band < nb - 1)
            def _():
                onward(c).start()

            save(c, 0).start()
            save(c, 1).start()
            gram(c)

        ahead = step + WINDOW

        @pl.when(ahead < chunks - wrapped)
        def _():
            prepare(ahead)

        @pl.when(ahead < chunks)
        def _():
            halo(ahead, 0).start()
            halo(ahead, 1).start()

    found = acc[...]
    found = found[: 2 * block] + found[2 * block :]
    found = found[:, :block] + found[:, block:]
    found = jnp.concatenate([found, jnp.zeros((2 * block, NZ - block), jnp.float32)], axis=1)
    part[...] = found
    for step in range(1, nd):
        total_to(step).start()
    parts[dom] = found
    for step in range(1, nd):
        total_from(step).wait_recv()
    summed = parts[0]
    for step in range(1, nd):
        summed = summed + parts[step]
    part_sum = summed

    @pl.loop(0, chunks)
    def _(c):
        halo(c, 0).wait_send()
        halo(c, 1).wait_send()
        save(c, 0).wait()
        save(c, 1).wait()

        @pl.when(band < nb - 1)
        def _():
            onward(c).wait_send()

    for step in range(1, nd):
        total_to(step).wait_send()
    part[...] = part_sum
    out = pltpu.make_async_copy(part, g_out, g_sem)
    out.start()
    out.wait()


def finish_kernel(count, planes, g_ref, a_ref, b_ref, o_ref, weights):
    block = a_ref.shape[1]
    rows = a_ref.shape[0]
    band = lax.axis_index("band")

    @pl.when(pl.program_id(0) == 0)
    def _():
        gram = g_ref[...] * (1.0 / count)
        corr = gram[:block, :block]
        cross = gram[block:, :block]
        row_id = lax.broadcasted_iota(jnp.int32, (block, block), 0)
        col_id = lax.broadcasted_iota(jnp.int32, (block, block), 1)
        work = jnp.concatenate([corr, jnp.where(row_id == col_id, 1.0, 0.0)], axis=1)
        row_of = lax.broadcasted_iota(jnp.int32, (block, 1), 0)
        for k in range(block):
            pivot = work[k : k + 1, :]
            factor = jnp.where(row_of > k, work[:, k : k + 1] / pivot[:, k : k + 1], 0.0)
            work = work - factor * pivot
        diagonal = jnp.where(row_id == col_id, work[:, :block], 0.0)
        norm = jnp.sqrt(jnp.sum(diagonal, axis=1, keepdims=True))
        inverse = jnp.where(col_id <= row_id, work[:, block:] / norm, 0.0)
        exact = dict(precision=lax.Precision.HIGHEST, preferred_element_type=jnp.float32)
        coeffs = lax.dot_general(cross, inverse, NT, **exact)
        mixed = jnp.dot(coeffs, inverse, **exact)
        chosen = jnp.where(band == 0, -inverse, mixed)
        high, low = split(chosen)
        weights[...] = jnp.concatenate([high, low, high, low], axis=1)

    keep = jnp.where(band == 0, 0.0, 1.0).astype(jnp.float32)
    lhs = weights[...]

    @pl.loop(0, rows // 8, unroll=4)
    def _(i):
        base = pl.multiple_of(i * 8, 8)
        cells = [base + p for p in range(8)]
        high, low = split(jnp.concatenate([b_ref[cell] for cell in cells], axis=1))
        rhs = jnp.concatenate([high, high, low, low], axis=0)
        change = jnp.dot(lhs, rhs, preferred_element_type=jnp.float32)
        fresh = [
            keep * a_ref[cell] - change[:, p * NZ : (p + 1) * NZ]
            for p, cell in enumerate(cells)
        ]
        o_ref[:, pl.ds(base, 8), :] = jnp.swapaxes(jnp.stack(fresh), 0, 1)


def body(orbitals, potential):
    block, planes, plane = orbitals.shape
    ny = plane // NZ
    rows = planes * ny
    nb, nd = lax.axis_size("band"), lax.axis_size("dom")
    chunk_count = ny // CHUNK_Y
    x = orbitals.reshape(block, planes, ny, NZ).transpose(0, 2, 1, 3).reshape(block, rows, NZ)
    v = potential.reshape(planes, ny, NZ).transpose(1, 0, 2).reshape(rows, NZ)
    cells = jax.ShapeDtypeStruct((rows, block, NZ), jnp.float32)
    cells_vmem = pltpu.VMEM((rows, block, NZ), jnp.float32)
    dma = pltpu.SemaphoreType.DMA
    hbm = pl.BlockSpec(memory_space=pl.ANY)
    applied, basis, gram = pl.pallas_call(
        functools.partial(apply_kernel, nb, nd, planes, ny),
        out_shape=(cells, cells, jax.ShapeDtypeStruct((2 * block, NZ), jnp.float32)),
        in_specs=[hbm, hbm],
        out_specs=(hbm, hbm, hbm),
        scratch_shapes=[
            pltpu.VMEM((block, rows, NZ), jnp.float32),
            cells_vmem, cells_vmem, cells_vmem, cells_vmem, cells_vmem,
            pltpu.VMEM((rows, NZ), jnp.float32),
            pltpu.VMEM((4 * block, 2 * block), jnp.float32),
            pltpu.VMEM((2 * block, NZ), jnp.float32),
            pltpu.VMEM((nd, 2 * block, NZ), jnp.float32),
            dma((chunk_count,)), dma((2, chunk_count)), dma((2, chunk_count)),
            dma((chunk_count,)), dma((chunk_count,)), dma((chunk_count,)), dma((chunk_count,)),
            dma((nd,)), dma((nd,)), dma, dma,
        ],
        compiler_params=pltpu.CompilerParams(
            collective_id=0, has_side_effects=True, vmem_limit_bytes=60 * MIB
        ),
        cost_estimate=pl.CostEstimate(
            flops=80 * block * rows * NZ, bytes_accessed=12 * block * rows * NZ, transcendentals=0
        ),
        name="apply_and_share",
    )(x, v)
    step_rows = 24 * planes
    count = rows * NZ * nd
    cell_spec = pl.BlockSpec((step_rows, block, NZ), lambda i: (i, 0, 0))
    result = pl.pallas_call(
        functools.partial(finish_kernel, count, planes),
        grid=(rows // step_rows,),
        out_shape=jax.ShapeDtypeStruct((block, rows, NZ), jnp.float32),
        in_specs=[pl.BlockSpec((2 * block, NZ), lambda i: (0, 0)), cell_spec, cell_spec],
        out_specs=pl.BlockSpec((block, step_rows, NZ), lambda i: (0, i, 0)),
        scratch_shapes=[pltpu.VMEM((block, 4 * block), jnp.bfloat16)],
        compiler_params=pltpu.CompilerParams(vmem_limit_bytes=60 * MIB),
        cost_estimate=pl.CostEstimate(
            flops=80 * block * rows * NZ, bytes_accessed=12 * block * rows * NZ, transcendentals=0
        ),
        name="finish",
    )(gram, applied, basis)
    result = result.reshape(block, ny, planes, NZ).transpose(0, 2, 1, 3)
    return result.reshape(block, planes, plane)


def solution(mesh):
    placed = (P("band", "dom", None), P("dom", None))
    return jax.shard_map(
        body, mesh=mesh, in_specs=placed, out_specs=P("band", "dom", None), check_vma=False
    )
```
